32 devices in a mesh: tpoint: 2 (over y), ao: 4 (over z), aux: 2 (over x), rep: 2 (over core).
Axes of the slice: x: 2, y: 2, z: 4, core: 2. Of those that a mesh axis runs over, the one named last changes fastest.
Arguments:
- tensor: bfloat16 [1024, 8, 4096], P(('aux', 'rep'), None, 'ao'), may hold values from -0.4375 to 0.4375
- block_mask: int32 [8, 8], replicated, may hold values 0 or 1
- occ_green: bfloat16 [16, 3, 64, 64], P(('tpoint', 'ao')), parts along dimension 0, may hold values from -0.75 to 0.75
- virt_green: bfloat16 [16, 3, 64, 64], P(('tpoint', 'ao')), parts along dimension 0, may hold values from -0.75 to 0.75
- green_mask: int32 [8, 3], replicated, may hold values 0 or 1
Outputs:
- response: float32 [512, 1024], P(('tpoint', 'ao'), ('aux', 'rep')), parts along dimension 0
The draws below stay inside these ranges and needn't reach their ends.
There are 2 independent parts, one for each index of `tpoint`. The reference program is written for one: setup_inputs(seed, part) draws one part's arguments, and reference() takes and returns one part's arrays. A program takes and returns all parts, laid end to end along the dimension named above; an argument that names none is the same for every part. Nothing has to cross between parts.
All inputs are finite; a program needn't handle non-finite values.
Results may differ from the reference program's by a relative error of at most 0.0041.
Values may be sent and summed in bfloat16 or wider, within the bound.
No kernel may reach another device: no remote copies, remote signals or barrier semaphores. Data moves between devices by JAX's collectives and lax.ppermute only.
A program may use at most 128 MiB of HBM per device.

```python
import jax
import jax.numpy as jnp
from jax import lax

AOB = 64
RB = 128
H = 1
SL = 64
K = 3
NB = 8
NRB = 8
NRI = 1024
RI_DEV = 256


def with_ends(entries, key, least, high):
    dims = entries.shape
    index_at = [jax.random.randint(jax.random.fold_in(key, axis), (), 0, dims[axis]) for axis in range(len(dims))]
    entries = entries.at[tuple(index_at)].set(least)
    longest = dims.index(max(dims))
    index_at[longest] = (index_at[longest] + 1) % dims[longest]
    return entries.at[tuple(index_at)].set(high)


def shard_levels(stream_key, extent, split, least, top_value):
    def one(axis_at, parts):
        steps = jax.random.uniform(jax.random.fold_in(jax.random.fold_in(stream_key, 6), axis_at), (parts,), jnp.float32, least / len(split), top_value / len(split))
        return jnp.repeat(jnp.exp(steps), extent[axis_at] // parts).reshape((-1,) + (1,) * (len(extent) - axis_at - 1))

    factor_of = one(*split[0])
    for cut in split[1:]:
        factor_of = factor_of * one(*cut)
    return factor_of


def normal_values(key, shape, width, limit, split=(), held_as=jnp.bfloat16):
    entries = jax.random.normal(key, shape, jnp.float32) * width
    if len(split) > 0:
        entries = shard_levels(key, shape, split, -0.22, 0.18) * entries
    return jnp.clip(entries, min=-limit, max=limit).astype(held_as)


def setup_inputs(seed: int = 0, part: int = 0) -> dict:
    keys = jax.random.split(jax.random.key(seed), 6)
    own_keys = jax.random.split(jax.random.fold_in(keys[5], part), 6)
    return {
        "tensor": normal_values(keys[0], (NRI, NB, AOB * AOB), ((NB * AOB * AOB) ** -0.25), 0.4375, ((0, 4), (2, 4))),
        "block_mask": with_ends((jax.random.randint(keys[1], (NRB, NB), 0, 4) < 3).astype(jnp.int32), jax.random.fold_in(keys[1], 1), 0, 1),
        "occ_green": normal_values(own_keys[2], (NB, K, AOB, AOB), AOB ** -0.5, 0.75, ((0, 4),)),
        "virt_green": normal_values(own_keys[3], (NB, K, AOB, AOB), AOB ** -0.5, 0.75, ((0, 4),)),
        "green_mask": with_ends((jax.random.randint(keys[4], (NB, K), 0, 4) < 3).astype(jnp.int32), jax.random.fold_in(keys[4], 1), 0, 1),
    }


def reference(tensor, block_mask, occ_green, virt_green, green_mask):
    blocks4 = tensor.reshape(NRI, NB, AOB, AOB)
    neighbour = jnp.arange(NB)[:, None] + jnp.arange(K)[None, :] - H
    valid = ((neighbour >= 0) & (neighbour < NB)).astype(jnp.int32)
    pair = (green_mask * valid).astype(jnp.float32)
    occ = occ_green.astype(jnp.float32) * pair[:, :, None, None]
    virt = virt_green.astype(jnp.float32) * pair[:, :, None, None]
    row_mask = jnp.repeat(block_mask, RB, axis=0).astype(jnp.float32)
    shards = NRI // RI_DEV
    slab_index = (jnp.arange(shards)[:, None] * RI_DEV + jnp.arange(SL)[None, :]).reshape(-1).astype(jnp.int32)
    slab = blocks4[slab_index].astype(jnp.float32) * row_mask[slab_index][:, :, None, None]
    padded = jnp.pad(slab, ((0, 0), (H, H), (0, 0), (0, 0)))

    def one_block(block):
        near = lax.dynamic_slice_in_dim(padded, block, K, 1)
        inner = jnp.einsum('pkmn,kns->pkms', near, virt[block])
        inner = lax.optimization_barrier(inner.astype(jnp.bfloat16)).astype(jnp.float32)
        summed = jnp.einsum('klm,pkms->pls', occ[block], inner)
        summed = lax.optimization_barrier(summed.astype(jnp.bfloat16)).astype(jnp.float32)
        column = lax.dynamic_index_in_dim(blocks4, block, 1, keepdims=False).astype(jnp.float32)
        weight = lax.dynamic_index_in_dim(row_mask, block, 1, keepdims=False)
        column = column * weight[:, None, None]
        return jnp.einsum('pls,qls->pq', summed, column)

    terms = lax.map(one_block, jnp.arange(NB).astype(jnp.int32))
    return jnp.sum(terms, axis=0)
```

```python
import jax
import jax.numpy as jnp
from jax import lax
from jax.sharding import PartitionSpec as P

AOB = 64
RB = 128
SL = 64


def green_blocks(occ_all, virt_all, green_mask, slab_mask):
    blocks, width = green_mask.shape
    reach = (width - 1) // 2
    neighbour = jnp.arange(blocks)[:, None] + jnp.arange(width)[None, :] - reach
    valid = (neighbour >= 0) & (neighbour < blocks)
    near_mask = slab_mask[jnp.clip(neighbour, 0, blocks - 1)]
    pair = jnp.where(valid, green_mask, 0)
    occ = occ_all * pair.astype(jnp.bfloat16)[:, :, None, None]
    virt = virt_all * (pair * near_mask).astype(jnp.bfloat16)[:, :, None, None]
    return occ, virt


def per_device(tensor, block_mask, occ_green, virt_green, green_mask):
    rows_dev, blocks, cols = tensor.shape
    reach = (occ_green.shape[1] - 1) // 2
    shard = lax.axis_index(("aux", "rep"))
    per_shard = rows_dev // RB
    mask_rows = lax.dynamic_slice_in_dim(block_mask, shard * per_shard, per_shard, 0)
    row_mask = jnp.repeat(mask_rows, RB, axis=0).astype(jnp.bfloat16)
    masked = tensor * row_mask[:, :, None]
    slab = lax.all_to_all(tensor[:SL], "ao", split_axis=0, concat_axis=2, tiled=True)
    occ_all = lax.all_gather(occ_green, "ao", axis=0, tiled=True)
    virt_all = lax.all_gather(virt_green, "ao", axis=0, tiled=True)
    occ, virt = green_blocks(occ_all, virt_all, green_mask, mask_rows[0])
    own = slab.shape[0]
    padded = jnp.pad(slab.reshape(own, blocks, AOB, AOB), ((0, 0), (reach, reach), (0, 0), (0, 0)))
    total = None
    for offset in range(2 * reach + 1):
        near = padded[:, offset : offset + blocks]
        inner = jnp.einsum(
            "rimn,ins->rims", near, virt[:, offset], preferred_element_type=jnp.float32
        ).astype(jnp.bfloat16)
        term = jnp.einsum(
            "ilm,rims->rils", occ[:, offset], inner, preferred_element_type=jnp.float32
        )
        total = term if total is None else total + term
    own_sums = total.astype(jnp.bfloat16).reshape(own, blocks, AOB * AOB)
    back = lax.all_to_all(own_sums, "ao", split_axis=2, concat_axis=0, tiled=True)
    sums = lax.all_gather(back, ("aux", "rep"), axis=0, tiled=True)
    partial_terms = lax.dot_general(
        sums, masked, (((1, 2), (1, 2)), ((), ())), preferred_element_type=jnp.float32
    )
    return lax.psum_scatter(partial_terms, "ao", scatter_dimension=0, tiled=True)


def solution(mesh):
    return jax.shard_map(
        per_device,
        mesh=mesh,
        in_specs=(
            P(("aux", "rep"), None, "ao"),
            P(),
            P(("tpoint", "ao"), None, None, None),
            P(("tpoint", "ao"), None, None, None),
            P(),
        ),
        out_specs=P(("tpoint", "ao"), ("aux", "rep")),
        check_vma=False,
    )
```

```python
import functools

import jax
import jax.numpy as jnp
from jax import lax
from jax.experimental import pallas as pl
from jax.experimental.pallas import tpu as pltpu
from jax.sharding import PartitionSpec as P

AOB = 64
RB = 128
SL = 64
LANES = 128
PAIR = LANES // AOB


def pair_masks(green_mask, slab_mask):
    blocks, width = green_mask.shape
    reach = (width - 1) // 2
    neighbour = jnp.arange(blocks)[:, None] + jnp.arange(width)[None, :] - reach
    valid = (neighbour >= 0) & (neighbour < blocks)
    near_mask = slab_mask[jnp.clip(neighbour, 0, blocks - 1)]
    pair = jnp.where(valid, green_mask, 0)
    return pair.astype(jnp.bfloat16), (pair * near_mask).astype(jnp.bfloat16)


def gathered_plan(tensor, masked, slab_mask, occ_green, virt_green, green_mask):
    blocks = tensor.shape[1]
    reach = (occ_green.shape[1] - 1) // 2
    slab = lax.all_to_all(tensor[:SL], "ao", split_axis=0, concat_axis=2, tiled=True)
    occ_all = lax.all_gather(occ_green, "ao", axis=0, tiled=True)
    virt_all = lax.all_gather(virt_green, "ao", axis=0, tiled=True)
    occ_mask, virt_mask = pair_masks(green_mask, slab_mask)
    occ = occ_all * occ_mask[:, :, None, None]
    virt = virt_all * virt_mask[:, :, None, None]
    own = slab.shape[0]
    padded = jnp.pad(slab.reshape(own, blocks, AOB, AOB), ((0, 0), (reach, reach), (0, 0), (0, 0)))
    total = None
    for offset in range(2 * reach + 1):
        near = padded[:, offset : offset + blocks]
        inner = jnp.einsum(
            "rimn,ins->rims", near, virt[:, offset], preferred_element_type=jnp.float32
        ).astype(jnp.bfloat16)
        term = jnp.einsum(
            "ilm,rims->rils", occ[:, offset], inner, preferred_element_type=jnp.float32
        )
        total = term if total is None else total + term
    own_sums = total.astype(jnp.bfloat16).reshape(own, blocks, AOB * AOB)
    back = lax.all_to_all(own_sums, "ao", split_axis=2, concat_axis=0, tiled=True)
    sums = lax.all_gather(back, ("aux", "rep"), axis=0, tiled=True)
    partial_terms = lax.dot_general(
        sums, masked, (((1, 2), (1, 2)), ((), ())), preferred_element_type=jnp.float32
    )
    return lax.psum_scatter(partial_terms, "ao", scatter_dimension=0, tiled=True)


def swap(value, axis, step):
    count = lax.axis_size(axis)
    return lax.ppermute(value, axis, [(i, i ^ step) for i in range(count)])


def contract_kernel(planes, *refs):
    chunks = refs[:planes]
    occ_ref, virt_ref = refs[planes : planes + 2]
    outs = refs[planes + 2 : 2 * planes + 2]
    even_ref, odd_ref, weight_ref, inner_ref, sums_ref = refs[2 * planes + 2 :]
    own, blocks, cols = chunks[0].shape
    width = virt_ref.shape[1]
    reach = (width - 1) // 2
    units = cols // LANES
    pairs = own // PAIR
    rows = planes * units
    f32 = jnp.float32
    for plane, chunk in enumerate(chunks):
        for p in range(own):
            value = chunk[p].astype(f32)
            target = even_ref if p % 2 == 0 else odd_ref
            for u in range(units):
                start = (p // 2) * rows + plane * units + u
                target[pl.ds(start, blocks, stride=pairs * rows), :] = value[
                    :, u * LANES : (u + 1) * LANES
                ]
    nothing = jnp.zeros((AOB, LANES), jnp.bfloat16)
    for m in range(blocks):
        for k in range(width):
            if not 0 <= m + k - reach < blocks:
                inner_ref[m, :, k * AOB : (k + 1) * AOB, :] = jnp.zeros(
                    (pairs // 2, AOB, 2 * LANES), jnp.bfloat16
                )
    for j in range(blocks):
        at = slice(j * pairs * rows, (j + 1) * pairs * rows)
        near = jnp.concatenate([even_ref[at, :], odd_ref[at, :]], axis=1).astype(jnp.bfloat16)
        for k in range(width):
            m = j + reach - k
            if not 0 <= m < blocks:
                continue
            for side in range(2):
                block = virt_ref[m, k, side]
                for half in range(2):
                    top = (side * 2 + half) * AOB
                    for out_half in range(2):
                        weight_ref[
                            j, k, top : top + AOB, out_half * LANES : (out_half + 1) * LANES
                        ] = block if half == out_half else nothing
            inner = jnp.dot(near, weight_ref[j, k], preferred_element_type=f32).astype(jnp.bfloat16)
            for pair in range(pairs):
                for half in range(2):
                    top = k * AOB + half * rows
                    inner_ref[
                        m,
                        pair // 2,
                        top : top + rows,
                        (pair % 2) * LANES : (pair % 2 + 1) * LANES,
                    ] = inner[pair * rows : (pair + 1) * rows, half * LANES : (half + 1) * LANES]
    low = lax.broadcasted_iota(jnp.int32, (rows, LANES), 1) < AOB
    for m in range(blocks):
        for group in range(pairs // 2):
            total = jnp.dot(occ_ref[m], inner_ref[m, group], preferred_element_type=f32)
            for side in range(2):
                lanes = slice(side * LANES, (side + 1) * LANES)
                first, second = total[:rows, lanes], total[rows:, lanes]
                even = jnp.where(low, first, pltpu.roll(second, AOB, 1))
                odd = jnp.where(low, pltpu.roll(first, AOB, 1), second)
                for part, value in enumerate((even, odd)):
                    p = (group * 2 + side) * 2 + part
                    for plane in range(planes):
                        start = (m * planes + plane) * units * own + p
                        sums_ref[pl.ds(start, units, stride=own), :] = value[
                            plane * units : (plane + 1) * units
                        ]
        for plane in range(planes):
            for u in range(units):
                start = ((m * planes + plane) * units + u) * own
                outs[plane][m, :, u * LANES : (u + 1) * LANES] = sums_ref[
                    start : start + own, :
                ].astype(jnp.bfloat16)


def contract(chunks, occ, virt):
    planes = len(chunks)
    own, blocks, cols = chunks[0].shape
    width = virt.shape[1]
    units = cols // LANES
    pairs = own // PAIR
    rows = planes * units
    whole = pl.BlockSpec(memory_space=pltpu.VMEM)
    flops = 2 * blocks * width * own * AOB * AOB * AOB * 4
    return pl.pallas_call(
        functools.partial(contract_kernel, planes),
        out_shape=[jax.ShapeDtypeStruct((blocks, own, cols), jnp.bfloat16)] * planes,
        in_specs=[whole] * (planes + 2),
        out_specs=[whole] * planes,
        scratch_shapes=[
            pltpu.VMEM((blocks * pairs * rows, LANES), jnp.float32),
            pltpu.VMEM((blocks * pairs * rows, LANES), jnp.float32),
            pltpu.VMEM((blocks, width, 2 * LANES, 2 * LANES), jnp.bfloat16),
            pltpu.VMEM((blocks, pairs // 2, width * AOB, 2 * LANES), jnp.bfloat16),
            pltpu.VMEM((blocks * rows * own, LANES), jnp.float32),
        ],
        compiler_params=pltpu.CompilerParams(vmem_limit_bytes=40 * 1024 * 1024),
        cost_estimate=pl.CostEstimate(flops=flops, bytes_accessed=3 << 20, transcendentals=0),
        name="contract_slab",
    )(*chunks, occ, virt)


def response_kernel(count, *refs):
    parts = refs[:count]
    masked_ref, out_ref = refs[count:]
    step = pl.program_id(0)

    @pl.when(step == 0)
    def _():
        out_ref[...] = jnp.zeros_like(out_ref)

    total = None
    for m in range(masked_ref.shape[0]):
        left = jnp.concatenate([part[m] for part in parts], axis=0)
        term = lax.dot_general(
            left, masked_ref[m], (((1,), (1,)), ((), ())), preferred_element_type=jnp.float32
        )
        total = term if total is None else total + term
    out_ref[...] += total


def response(parts, masked):
    blocks, own, cols = parts[0].shape
    rows_dev = masked.shape[1]
    count = len(parts)
    per_step = 2
    return pl.pallas_call(
        functools.partial(response_kernel, count),
        grid=(blocks // per_step,),
        out_shape=jax.ShapeDtypeStruct((count * own, rows_dev), jnp.float32),
        in_specs=[pl.BlockSpec((per_step, own, cols), lambda s: (s, 0, 0))] * count
        + [pl.BlockSpec((per_step, rows_dev, cols), lambda s: (s, 0, 0))],
        out_specs=pl.BlockSpec((count * own, rows_dev), lambda s: (0, 0)),
        compiler_params=pltpu.CompilerParams(vmem_limit_bytes=24 * 1024 * 1024),
        cost_estimate=pl.CostEstimate(
            flops=2 * count * own * rows_dev * blocks * cols,
            bytes_accessed=2 * rows_dev * blocks * cols,
            transcendentals=0,
        ),
        name="response_terms",
    )(*parts, masked)


def swapped_plan(tensor, masked, slab_mask, occ_green, virt_green, green_mask):
    planes = lax.axis_size("ao")
    steps = range(1, planes)
    z = lax.axis_index("ao")
    core = lax.axis_index("rep")
    shard = lax.axis_index(("aux", "rep"))
    own = SL // planes
    cols = tensor.shape[2]
    units = cols // LANES
    blocks = tensor.shape[1]

    def rows_of(plane):
        return lax.dynamic_slice_in_dim(tensor, plane * own, own, 0)

    chunks = [rows_of(z)] + [swap(rows_of(z ^ k), "ao", k) for k in steps]
    mine = jnp.where(core == 0, occ_green, virt_green)
    stacked = jnp.stack([mine] + [swap(mine, "ao", k) for k in steps])
    order = jnp.arange(planes) ^ z
    mine_all = stacked[order].reshape((blocks,) + mine.shape[1:])
    other_all = swap(mine_all, "rep", 1)
    occ_mask, virt_mask = pair_masks(green_mask, slab_mask)
    occ = jnp.where(core == 0, mine_all, other_all) * occ_mask[:, :, None, None]
    virt = jnp.where(core == 0, other_all, mine_all) * virt_mask[:, :, None, None]
    place = jnp.arange(AOB)
    source = (
        (z ^ (place // units % planes)) * (AOB // planes)
        + PAIR * (place % units)
        + place // (planes * units)
    )
    select = (source[:, None] == jnp.arange(AOB)[None, :]).astype(jnp.bfloat16)
    occ = jnp.einsum("ai,mkij->mkaj", select, occ)
    occ = jnp.einsum("mkaj,bj->makb", occ, select).reshape(blocks, AOB, -1)
    virt = jnp.stack(
        [
            jnp.pad(virt, ((0, 0), (0, 0), (0, 0), (0, LANES - AOB))),
            jnp.pad(virt, ((0, 0), (0, 0), (0, 0), (LANES - AOB, 0))),
        ],
        axis=2,
    )
    sums = contract(chunks, occ, virt)
    terms = []
    for k in range(planes):
        near = sums[k] if k == 0 else swap(sums[k], "ao", k)
        far = swap(near, "aux", 1)
        terms.append(
            response([near, swap(near, "rep", 1), far, swap(far, "rep", 1)], masked).reshape(
                planes, own, -1
            )
        )
    terms = jnp.stack(terms)

    def block_for(k):
        kept = lax.dynamic_index_in_dim(terms, shard ^ z ^ k, 1, keepdims=False)
        return jnp.stack([kept[p ^ k] for p in range(planes)])

    total = block_for(0)
    for k in steps:
        total = total + swap(block_for(k).astype(jnp.bfloat16), "ao", k).astype(jnp.float32)
    return total[order].reshape(SL, -1)


def per_device(tensor, block_mask, occ_green, virt_green, green_mask):
    rows_dev, blocks, cols = tensor.shape
    shard = lax.axis_index(("aux", "rep"))
    per_shard = rows_dev // RB
    mask_rows = lax.dynamic_slice_in_dim(block_mask, shard * per_shard, per_shard, 0)
    row_mask = jnp.repeat(mask_rows, RB, axis=0).astype(jnp.bfloat16)
    planes = lax.axis_size("ao")
    simple = planes == 4 and lax.axis_size("aux") == 2 and lax.axis_size("rep") == 2
    if simple and cols * planes == AOB * AOB and SL // planes % 16 == 0:
        masked = jnp.swapaxes(tensor, 0, 1) * row_mask.T[:, :, None]
        plan = swapped_plan
    else:
        masked = tensor * row_mask[:, :, None]
        plan = gathered_plan
    return plan(tensor, masked, mask_rows[0], occ_green, virt_green, green_mask)


def solution(mesh):
    return jax.shard_map(
        per_device,
        mesh=mesh,
        in_specs=(
            P(("aux", "rep"), None, "ao"),
            P(),
            P(("tpoint", "ao"), None, None, None),
            P(("tpoint", "ao"), None, None, None),
            P(),
        ),
        out_specs=P(("tpoint", "ao"), ("aux", "rep")),
        check_vma=False,
    )
```

```python
import functools

import jax
import jax.numpy as jnp
from jax import lax
from jax.experimental import pallas as pl
from jax.experimental.pallas import tpu as pltpu
from jax.sharding import PartitionSpec as P

AOB = 64
RB = 128
SL = 64
LANES = 128
PAIR = LANES // AOB
TINY = pl.CostEstimate(flops=1, bytes_accessed=1, transcendentals=0)


def pair_masks(green_mask, slab_mask):
    blocks, width = green_mask.shape
    reach = (width - 1) // 2
    neighbour = jnp.arange(blocks)[:, None] + jnp.arange(width)[None, :] - reach
    valid = (neighbour >= 0) & (neighbour < blocks)
    near_mask = slab_mask[jnp.clip(neighbour, 0, blocks - 1)]
    pair = jnp.where(valid, green_mask, 0)
    return pair.astype(jnp.bfloat16), (pair * near_mask).astype(jnp.bfloat16)


def gathered_plan(tensor, mask_rows, occ_green, virt_green, green_mask):
    blocks = tensor.shape[1]
    row_mask = jnp.repeat(mask_rows, RB, axis=0).astype(jnp.bfloat16)
    masked = tensor * row_mask[:, :, None]
    reach = (occ_green.shape[1] - 1) // 2
    slab = lax.all_to_all(tensor[:SL], "ao", split_axis=0, concat_axis=2, tiled=True)
    occ_all = lax.all_gather(occ_green, "ao", axis=0, tiled=True)
    virt_all = lax.all_gather(virt_green, "ao", axis=0, tiled=True)
    occ_mask, virt_mask = pair_masks(green_mask, mask_rows[0])
    occ = occ_all * occ_mask[:, :, None, None]
    virt = virt_all * virt_mask[:, :, None, None]
    own = slab.shape[0]
    padded = jnp.pad(slab.reshape(own, blocks, AOB, AOB), ((0, 0), (reach, reach), (0, 0), (0, 0)))
    total = None
    for offset in range(2 * reach + 1):
        near = padded[:, offset : offset + blocks]
        inner = jnp.einsum(
            "rimn,ins->rims", near, virt[:, offset], preferred_element_type=jnp.float32
        ).astype(jnp.bfloat16)
        term = jnp.einsum(
            "ilm,rims->rils", occ[:, offset], inner, preferred_element_type=jnp.float32
        )
        total = term if total is None else total + term
    own_sums = total.astype(jnp.bfloat16).reshape(own, blocks, AOB * AOB)
    back = lax.all_to_all(own_sums, "ao", split_axis=2, concat_axis=0, tiled=True)
    sums = lax.all_gather(back, ("aux", "rep"), axis=0, tiled=True)
    partial_terms = lax.dot_general(
        sums, masked, (((1, 2), (1, 2)), ((), ())), preferred_element_type=jnp.float32
    )
    return lax.psum_scatter(partial_terms, "ao", scatter_dimension=0, tiled=True)


def swap(value, axis, step):
    count = lax.axis_size(axis)
    return lax.ppermute(value, axis, [(i, i ^ step) for i in range(count)])


def contract_kernel(planes, *refs):
    halves = refs[: 2 * planes]
    occ_ref, virt_ref = refs[2 * planes : 2 * planes + 2]
    outs = refs[2 * planes + 2 : 3 * planes + 2]
    even_ref, odd_ref, weight_ref, inner_ref, sums_ref = refs[3 * planes + 2 :]
    blocks, own, cols = outs[0].shape
    width = virt_ref.shape[1]
    reach = (width - 1) // 2
    units = cols // LANES
    pairs = own // PAIR
    rows = planes * units
    f32 = jnp.float32
    for plane in range(planes):
        for p in range(own):
            half = halves[2 * plane + p // (own // 2)]
            value = half[p % (own // 2)].astype(f32)
            target = even_ref if p % 2 == 0 else odd_ref
            for u in range(units):
                start = (p // 2) * rows + plane * units + u
                target[pl.ds(start, blocks, stride=pairs * rows), :] = value[
                    :, u * LANES : (u + 1) * LANES
                ]
    nothing = jnp.zeros((AOB, LANES), jnp.bfloat16)
    for m in range(blocks):
        for k in range(width):
            if not 0 <= m + k - reach < blocks:
                inner_ref[m, :, k * AOB : (k + 1) * AOB, :] = jnp.zeros(
                    (pairs // 2, AOB, 2 * LANES), jnp.bfloat16
                )
    for j in range(blocks):
        at = slice(j * pairs * rows, (j + 1) * pairs * rows)
        near = jnp.concatenate([even_ref[at, :], odd_ref[at, :]], axis=1).astype(jnp.bfloat16)
        for k in range(width):
            m = j + reach - k
            if not 0 <= m < blocks:
                continue
            for side in range(2):
                block = virt_ref[m, k, side]
                for half in range(2):
                    top = (side * 2 + half) * AOB
                    for out_half in range(2):
                        weight_ref[
                            j, k, top : top + AOB, out_half * LANES : (out_half + 1) * LANES
                        ] = block if half == out_half else nothing
            inner = jnp.dot(near, weight_ref[j, k], preferred_element_type=f32).astype(jnp.bfloat16)
            for pair in range(pairs):
                for half in range(2):
                    top = k * AOB + half * rows
                    inner_ref[
                        m,
                        pair // 2,
                        top : top + rows,
                        (pair % 2) * LANES : (pair % 2 + 1) * LANES,
                    ] = inner[pair * rows : (pair + 1) * rows, half * LANES : (half + 1) * LANES]
    low = lax.broadcasted_iota(jnp.int32, (rows, LANES), 1) < AOB
    for m in range(blocks):
        for group in range(pairs // 2):
            total = jnp.dot(occ_ref[m], inner_ref[m, group], preferred_element_type=f32)
            for side in range(2):
                lanes = slice(side * LANES, (side + 1) * LANES)
                first, second = total[:rows, lanes], total[rows:, lanes]
                even = jnp.where(low, first, pltpu.roll(second, AOB, 1))
                odd = jnp.where(low, pltpu.roll(first, AOB, 1), second)
                for part, value in enumerate((even, odd)):
                    p = (group * 2 + side) * 2 + part
                    for plane in range(planes):
                        start = (m * planes + plane) * units * own + p
                        sums_ref[pl.ds(start, units, stride=own), :] = value[
                            plane * units : (plane + 1) * units
                        ]
        for plane in range(planes):
            for u in range(units):
                start = ((m * planes + plane) * units + u) * own
                outs[plane][m, :, u * LANES : (u + 1) * LANES] = sums_ref[
                    start : start + own, :
                ].astype(jnp.bfloat16)


def contract(halves, occ, virt):
    planes = len(halves) // 2
    half, blocks, cols = halves[1].shape
    own = 2 * half
    width = virt.shape[1]
    units = cols // LANES
    pairs = own // PAIR
    rows = planes * units
    whole = pl.BlockSpec(memory_space=pltpu.VMEM)
    return pl.pallas_call(
        functools.partial(contract_kernel, planes),
        out_shape=[jax.ShapeDtypeStruct((blocks, own, cols), jnp.bfloat16)] * planes,
        in_specs=[whole] * (2 * planes + 2),
        out_specs=[whole] * planes,
        scratch_shapes=[
            pltpu.VMEM((blocks * pairs * rows, LANES), jnp.float32),
            pltpu.VMEM((blocks * pairs * rows, LANES), jnp.float32),
            pltpu.VMEM((blocks, width, 2 * LANES, 2 * LANES), jnp.bfloat16),
            pltpu.VMEM((blocks, pairs // 2, width * AOB, 2 * LANES), jnp.bfloat16),
            pltpu.VMEM((blocks * rows * own, LANES), jnp.float32),
        ],
        compiler_params=pltpu.CompilerParams(vmem_limit_bytes=20 * 1024 * 1024),
        cost_estimate=TINY,
        name="contract_slab",
    )(*halves, occ, virt)


def add_terms(k, near, far, rows_ref, keep_ref, core, cross_refs, into_ref):
    blocks, own, cols = near.shape
    rows = rows_ref.shape[0] // blocks
    right = jnp.concatenate(
        [near[...].reshape(blocks * own, cols), far[...].reshape(blocks * own, cols)], axis=0
    )
    some = 64
    group = lax.broadcasted_iota(jnp.int32, (some, LANES), 1) // own
    for part in range(rows // some):
        cross = lax.dot_general(
            rows_ref[part * some * blocks : (part + 1) * some * blocks, :],
            right,
            (((1,), (1,)), ((), ())),
            preferred_element_type=jnp.float32,
        )
        keep = keep_ref[core, part * some // RB][None, :]
        for side in range(2):
            hold = cross_refs.at[part % 2, side]
            hold[...] = cross[:, side * LANES : (side + 1) * LANES]
            total = hold[pl.ds(0, some, stride=blocks), :]
            for m in range(1, blocks):
                total = jnp.where(group == m, hold[pl.ds(m, some, stride=blocks), :], total)
            total = total * keep
            shift = LANES // 2
            while shift >= own:
                total = total + pltpu.roll(total, shift, 1)
                shift //= 2
            at = slice(part * some, (part + 1) * some)
            into_ref[core, at, :] = jnp.where(
                group == 2 * k + side, total, into_ref[core, at, :]
            )


def first_kernel(count, keep_ref, *refs):
    parts, sources = refs[: 2 * count], refs[2 * count : 2 * count + 2]
    out_ref, *kept = refs[2 * count + 2 : 2 * count + 5]
    cross_refs, sem = refs[2 * count + 5 :]
    copies = [pltpu.make_async_copy(sources[c], kept[c], sem.at[c]) for c in range(2)]
    for copy in copies:
        copy.start()
    out_ref[...] = jnp.zeros_like(out_ref)
    for core in range(2):
        copies[core].wait()
        for k in range(count):
            add_terms(k, parts[2 * k], parts[2 * k + 1], kept[core], keep_ref, core, cross_refs, out_ref)


def next_kernel(k, keep_ref, near_ref, far_ref, own_ref, other_ref, early_ref, out_ref, cross_refs):
    out_ref[...] = early_ref[...]
    for core, rows_ref in enumerate((own_ref, other_ref)):
        add_terms(k, near_ref, far_ref, rows_ref, keep_ref, core, cross_refs, out_ref)


def last_kernel(
    place_ref, keep_ref, near_ref, far_ref, own_ref, other_ref, early_ref, out_ref, hold_ref, turn_ref, cross_refs
):
    count, own = out_ref.shape[0], near_ref.shape[1]
    hold_ref[...] = early_ref[...]
    for core, rows_ref in enumerate((own_ref, other_ref)):
        add_terms(count - 1, near_ref, far_ref, rows_ref, keep_ref, core, cross_refs, hold_ref)
        turn_ref[core] = hold_ref[core].T
    for route in range(count):
        side, core = place_ref[0] ^ (route // 2), place_ref[1] ^ (route % 2)
        for p in range(count):
            start = pl.multiple_of((2 * (p ^ route) + side) * own, own)
            out_ref[route, p * own : (p + 1) * own, :] = turn_ref[
                core, pl.ds(start, own), :
            ].astype(jnp.bfloat16)


WHOLE = pl.BlockSpec(memory_space=pltpu.VMEM)
PARAMS = pltpu.CompilerParams(vmem_limit_bytes=20 * 1024 * 1024)


def cross_scratch(blocks):
    return pltpu.VMEM((2, 2, 64 * blocks, LANES), jnp.float32)


def first_terms(keep, parts, sources):
    blocks, own, cols = parts[0].shape
    rows = sources[0].shape[0]
    return pl.pallas_call(
        functools.partial(first_kernel, len(parts) // 2),
        out_shape=[jax.ShapeDtypeStruct((2, rows // blocks, LANES), jnp.float32)]
        + [pltpu.VMEM((rows, cols), jnp.bfloat16)] * 2,
        in_specs=[WHOLE] * (len(parts) + 1) + [pl.BlockSpec(memory_space=pl.ANY)] * 2,
        out_specs=[WHOLE] * 3,
        scratch_shapes=[cross_scratch(blocks), pltpu.SemaphoreType.DMA((2,))],
        compiler_params=PARAMS,
        cost_estimate=TINY,
        name="first_terms",
    )(keep, *parts, *sources)


def next_terms(k, keep, near, far, rows, early):
    return pl.pallas_call(
        functools.partial(next_kernel, k),
        out_shape=jax.ShapeDtypeStruct(early.shape, jnp.float32),
        in_specs=[WHOLE] * 6,
        out_specs=WHOLE,
        scratch_shapes=[cross_scratch(near.shape[0])],
        compiler_params=PARAMS,
        cost_estimate=TINY,
        name="next_terms",
    )(keep, near, far, *rows, early)


def last_terms(place, keep, near, far, rows, early):
    own = near.shape[1]
    rows_dev = early.shape[1]
    count = LANES // (2 * own)
    return pl.pallas_call(
        last_kernel,
        out_shape=jax.ShapeDtypeStruct((count, count * own, rows_dev), jnp.bfloat16),
        in_specs=[pl.BlockSpec(memory_space=pltpu.SMEM)] + [WHOLE] * 6,
        out_specs=WHOLE,
        scratch_shapes=[
            pltpu.VMEM(early.shape, jnp.float32),
            pltpu.VMEM((2, LANES, rows_dev), jnp.float32),
            cross_scratch(near.shape[0]),
        ],
        compiler_params=PARAMS,
        cost_estimate=TINY,
        name="last_terms",
    )(place, keep, near, far, *rows, early)


def routed(value, route):
    pairs = []
    for z in range(4):
        for core in range(2):
            to_z = 2 * ((z // 2) ^ (route // 2)) + core
            to_core = (z % 2) ^ (route % 2)
            pairs.append((2 * z + core, 2 * to_z + to_core))
    return lax.ppermute(value, ("ao", "rep"), pairs)


def after(value, *others):
    return lax.optimization_barrier((value,) + others)[0]


def swapped_plan(tensor, mask_rows, other_mask_rows, occ_green, virt_green, green_mask):
    planes = lax.axis_size("ao")
    steps = range(1, planes)
    z = lax.axis_index("ao")
    core = lax.axis_index("rep")
    aux = lax.axis_index("aux")
    side = lax.axis_index("tpoint")
    own = SL // planes
    half = own // 2
    rows_dev, blocks, cols = tensor.shape
    units = cols // LANES

    def rows_of(plane, part):
        return lax.dynamic_slice_in_dim(tensor, plane * own + part * half, half, 0)

    mine = jnp.where(core == 0, occ_green, virt_green).reshape(-1, blocks, cols)
    leaving = [jnp.concatenate([rows_of(z ^ k, side), mine]) for k in steps]
    direct = [swap(leaving[k - 1], "ao", k) for k in steps]
    halves = [rows_of(z, side), rows_of(z, 1 - side)]
    for value in direct:
        halves += [value, swap(value[:half], "tpoint", 1)]
    stacked = jnp.stack([mine] + [value[half:] for value in direct])
    order = jnp.arange(planes) ^ z
    other = swap(stacked, "rep", 1)
    shape = (blocks,) + occ_green.shape[1:]
    mine_all = stacked[order].reshape(shape)
    other_all = other[order].reshape(shape)
    rows = tensor.reshape(rows_dev * blocks, cols)
    rows = (rows, swap(rows, "rep", 1))
    occ_mask, virt_mask = pair_masks(green_mask, mask_rows[0])
    occ = jnp.where(core == 0, mine_all, other_all) * occ_mask[:, :, None, None]
    virt = jnp.where(core == 0, other_all, mine_all) * virt_mask[:, :, None, None]
    place = jnp.arange(AOB)
    source = (
        (z ^ (place // units % planes)) * (AOB // planes)
        + PAIR * (place % units)
        + place // (planes * units)
    )
    select = (source[:, None] == jnp.arange(AOB)[None, :]).astype(jnp.bfloat16)
    occ = jnp.einsum("ai,mkij->mkaj", select, occ)
    occ = jnp.einsum("mkaj,bj->makb", occ, select).reshape(blocks, AOB, -1)
    virt = jnp.stack(
        [
            jnp.pad(virt, ((0, 0), (0, 0), (0, 0), (0, LANES - AOB))),
            jnp.pad(virt, ((0, 0), (0, 0), (0, 0), (LANES - AOB, 0))),
        ],
        axis=2,
    )
    sums = contract(halves, occ, virt)
    near = [sums[0], swap(sums[1], "ao", 1), swap(sums[2], "ao", 2)]
    near.append(swap(after(sums[3], near[1]), "ao", 3))
    far = [swap(value, "aux", 1) for value in (sums[0], sums[1], near[2], near[3])]
    far[1] = swap(far[1], "ao", 1)
    keep = jnp.repeat(jnp.stack([mask_rows, other_mask_rows]), own, axis=2).astype(jnp.float32)
    early, *rows = first_terms(keep, [near[0], far[0], near[1], far[1]], rows)
    early = next_terms(2, keep, near[2], far[2], rows, early)
    place = jnp.stack([(z // 2) ^ aux, (z % 2) ^ core]).astype(jnp.int32)
    leaving = last_terms(place, keep, near[3], far[3], rows, early)
    total = None
    for route in range(planes):
        term = routed(leaving[route], route).astype(jnp.float32)
        total = term if total is None else total + term
    index = jnp.arange(2 * planes)
    home = index ^ (2 * (2 * (z // 2) + core) + side)
    return total.reshape(2 * planes, half, -1)[home].reshape(SL, -1)


def per_device(tensor, block_mask, occ_green, virt_green, green_mask):
    rows_dev, blocks, cols = tensor.shape
    shard = lax.axis_index(("aux", "rep"))
    per_shard = rows_dev // RB
    planes = lax.axis_size("ao")

    def mask_of(index):
        return lax.dynamic_slice_in_dim(block_mask, index * per_shard, per_shard, 0)

    sizes = tuple(lax.axis_size(axis) for axis in ("tpoint", "ao", "aux", "rep"))
    simple = sizes == (2, 4, 2, 2) and cols * planes == AOB * AOB and SL // planes == 16
    simple = simple and blocks * 16 == LANES and rows_dev % RB == 0 and occ_green.shape[1] == 3
    if simple:
        return swapped_plan(
            tensor, mask_of(shard), mask_of(shard ^ 1), occ_green, virt_green, green_mask
        )
    return gathered_plan(tensor, mask_of(shard), occ_green, virt_green, green_mask)


def solution(mesh):
    return jax.shard_map(
        per_device,
        mesh=mesh,
        in_specs=(
            P(("aux", "rep"), None, "ao"),
            P(),
            P(("tpoint", "ao"), None, None, None),
            P(("tpoint", "ao"), None, None, None),
            P(),
        ),
        out_specs=P(("tpoint", "ao"), ("aux", "rep")),
        check_vma=False,
    )
```

```python
import functools

import jax
import jax.numpy as jnp
from jax import lax
from jax.experimental import pallas as pl
from jax.experimental.pallas import tpu as pltpu
from jax.sharding import PartitionSpec as P

AOB = 64
RB = 128
SL = 64
LANES = 128
PAIR = LANES // AOB
TINY = pl.CostEstimate(flops=1, bytes_accessed=1, transcendentals=0)


def pair_masks(green_mask, slab_mask):
    blocks, width = green_mask.shape
    reach = (width - 1) // 2
    neighbour = jnp.arange(blocks)[:, None] + jnp.arange(width)[None, :] - reach
    valid = (neighbour >= 0) & (neighbour < blocks)
    near_mask = slab_mask[jnp.clip(neighbour, 0, blocks - 1)]
    pair = jnp.where(valid, green_mask, 0)
    return pair.astype(jnp.bfloat16), (pair * near_mask).astype(jnp.bfloat16)


def gathered_plan(tensor, mask_rows, occ_green, virt_green, green_mask):
    blocks = tensor.shape[1]
    row_mask = jnp.repeat(mask_rows, RB, axis=0).astype(jnp.bfloat16)
    masked = tensor * row_mask[:, :, None]
    reach = (occ_green.shape[1] - 1) // 2
    slab = lax.all_to_all(tensor[:SL], "ao", split_axis=0, concat_axis=2, tiled=True)
    occ_all = lax.all_gather(occ_green, "ao", axis=0, tiled=True)
    virt_all = lax.all_gather(virt_green, "ao", axis=0, tiled=True)
    occ_mask, virt_mask = pair_masks(green_mask, mask_rows[0])
    occ = occ_all * occ_mask[:, :, None, None]
    virt = virt_all * virt_mask[:, :, None, None]
    own = slab.shape[0]
    padded = jnp.pad(slab.reshape(own, blocks, AOB, AOB), ((0, 0), (reach, reach), (0, 0), (0, 0)))
    total = None
    for offset in range(2 * reach + 1):
        near = padded[:, offset : offset + blocks]
        inner = jnp.einsum(
            "rimn,ins->rims", near, virt[:, offset], preferred_element_type=jnp.float32
        ).astype(jnp.bfloat16)
        term = jnp.einsum(
            "ilm,rims->rils", occ[:, offset], inner, preferred_element_type=jnp.float32
        )
        total = term if total is None else total + term
    own_sums = total.astype(jnp.bfloat16).reshape(own, blocks, AOB * AOB)
    back = lax.all_to_all(own_sums, "ao", split_axis=2, concat_axis=0, tiled=True)
    sums = lax.all_gather(back, ("aux", "rep"), axis=0, tiled=True)
    partial_terms = lax.dot_general(
        sums, masked, (((1, 2), (1, 2)), ((), ())), preferred_element_type=jnp.float32
    )
    return lax.psum_scatter(partial_terms, "ao", scatter_dimension=0, tiled=True)


def swap(value, axis, step):
    count = lax.axis_size(axis)
    return lax.ppermute(value, axis, [(i, i ^ step) for i in range(count)])


def contract_kernel(planes, part_ref, *refs):
    pieces = refs[: 2 * planes - 2]
    occ_ref, virt_ref = refs[2 * planes - 2 : 2 * planes]
    outs = refs[2 * planes : 3 * planes + 1]
    even_ref, odd_ref, weight_ref, inner_ref, sums_ref = refs[3 * planes + 1 :]
    blocks, own, cols = outs[0].shape
    width = virt_ref.shape[1]
    reach = (width - 1) // 2
    units = cols // LANES
    pairs = own // PAIR
    rows = planes * units
    f32 = jnp.float32
    for plane in range(planes):
        for p in range(own):
            if plane < 2:
                piece, at = pieces[plane], part_ref[0] * (own // 2) ^ p
            else:
                piece, at = pieces[2 * plane - 2 + p // (own // 2)], p % (own // 2)
            value = piece[at].astype(f32)
            target = even_ref if p % 2 == 0 else odd_ref
            for u in range(units):
                start = (p // 2) * rows + plane * units + u
                target[pl.ds(start, blocks, stride=pairs * rows), :] = value[
                    :, u * LANES : (u + 1) * LANES
                ]
    nothing = jnp.zeros((AOB, LANES), jnp.bfloat16)
    for m in range(blocks):
        for k in range(width):
            if not 0 <= m + k - reach < blocks:
                inner_ref[m, :, k * AOB : (k + 1) * AOB, :] = jnp.zeros(
                    (pairs // 2, AOB, 2 * LANES), jnp.bfloat16
                )
    for j in range(blocks):
        at = slice(j * pairs * rows, (j + 1) * pairs * rows)
        near = jnp.concatenate([even_ref[at, :], odd_ref[at, :]], axis=1).astype(jnp.bfloat16)
        for k in range(width):
            m = j + reach - k
            if not 0 <= m < blocks:
                continue
            for side in range(2):
                block = virt_ref[m, k, side]
                for half in range(2):
                    top = (side * 2 + half) * AOB
                    for out_half in range(2):
                        weight_ref[
                            j, k, top : top + AOB, out_half * LANES : (out_half + 1) * LANES
                        ] = block if half == out_half else nothing
            inner = jnp.dot(near, weight_ref[j, k], preferred_element_type=f32).astype(jnp.bfloat16)
            for pair in range(pairs):
                for half in range(2):
                    top = k * AOB + half * rows
                    inner_ref[
                        m,
                        pair // 2,
                        top : top + rows,
                        (pair % 2) * LANES : (pair % 2 + 1) * LANES,
                    ] = inner[pair * rows : (pair + 1) * rows, half * LANES : (half + 1) * LANES]
    low = lax.broadcasted_iota(jnp.int32, (rows, LANES), 1) < AOB
    for m in range(blocks):
        for group in range(pairs // 2):
            total = jnp.dot(occ_ref[m], inner_ref[m, group], preferred_element_type=f32)
            for side in range(2):
                lanes = slice(side * LANES, (side + 1) * LANES)
                first, second = total[:rows, lanes], total[rows:, lanes]
                even = jnp.where(low, first, pltpu.roll(second, AOB, 1))
                odd = jnp.where(low, pltpu.roll(first, AOB, 1), second)
                for part, value in enumerate((even, odd)):
                    p = (group * 2 + side) * 2 + part
                    for plane in range(planes):
                        start = (m * planes + plane) * units * own + p
                        sums_ref[pl.ds(start, units, stride=own), :] = value[
                            plane * units : (plane + 1) * units
                        ]
        for plane in range(planes):
            for u in range(units):
                start = ((m * planes + plane) * units + u) * own
                into, at = outs[plane], m
                if plane == planes - 1 and m >= blocks // 2:
                    into, at = outs[planes], m - blocks // 2
                into[at, :, u * LANES : (u + 1) * LANES] = sums_ref[
                    start : start + own, :
                ].astype(jnp.bfloat16)


def contract(part, pieces, occ, virt):
    planes = len(pieces) // 2 + 1
    own, blocks, cols = pieces[0].shape
    width = virt.shape[1]
    units = cols // LANES
    pairs = own // PAIR
    rows = planes * units
    whole = pl.BlockSpec(memory_space=pltpu.VMEM)
    return pl.pallas_call(
        functools.partial(contract_kernel, planes),
        out_shape=[jax.ShapeDtypeStruct((blocks, own, cols), jnp.bfloat16)] * (planes - 1)
        + [jax.ShapeDtypeStruct((blocks // 2, own, cols), jnp.bfloat16)] * 2,
        in_specs=[pl.BlockSpec(memory_space=pltpu.SMEM)] + [whole] * (2 * planes),
        out_specs=[whole] * (planes + 1),
        scratch_shapes=[
            pltpu.VMEM((blocks * pairs * rows, LANES), jnp.float32),
            pltpu.VMEM((blocks * pairs * rows, LANES), jnp.float32),
            pltpu.VMEM((blocks, width, 2 * LANES, 2 * LANES), jnp.bfloat16),
            pltpu.VMEM((blocks, pairs // 2, width * AOB, 2 * LANES), jnp.bfloat16),
            pltpu.VMEM((blocks * rows * own, LANES), jnp.float32),
        ],
        compiler_params=pltpu.CompilerParams(vmem_limit_bytes=20 * 1024 * 1024),
        cost_estimate=TINY,
        name="contract_slab",
    )(part.reshape(1), *pieces, occ, virt)


def product(right, masked_ref):
    total = None
    for m in range(masked_ref.shape[0]):
        term = lax.dot_general(
            masked_ref[m], right[m], (((1,), (1,)), ((), ())), preferred_element_type=jnp.float32
        )
        total = term if total is None else total + term
    return total


WHOLE = pl.BlockSpec(memory_space=pltpu.VMEM)
SMALL = pltpu.CompilerParams(vmem_limit_bytes=16 * 1024 * 1024)


def early_kernel(count, *refs):
    parts, masked_refs, out_ref = refs[:count], refs[count : count + 2], refs[count + 2]
    blocks, own, cols = parts[0].shape
    nothing = jnp.zeros((LANES - count * own, cols), jnp.bfloat16)
    right = []
    for m in range(blocks):
        right.append(jnp.concatenate([part[m] for part in parts] + [nothing], axis=0))
    for core in range(2):
        out_ref[core] = product(right, masked_refs[core])


def early_terms(parts, masked):
    rows_dev = masked[0].shape[1]
    return pl.pallas_call(
        functools.partial(early_kernel, len(parts)),
        out_shape=jax.ShapeDtypeStruct((2, rows_dev, LANES), jnp.float32),
        in_specs=[WHOLE] * (len(parts) + 2),
        out_specs=WHOLE,
        compiler_params=SMALL,
        cost_estimate=TINY,
        name="early_terms",
    )(*parts, *masked)


def final_kernel(place_ref, *refs):
    near, far = refs[:2], refs[2:4]
    own_ref, other_ref, early_ref, out_ref, hold_ref = refs[4:]
    count = out_ref.shape[0]
    part, own, cols = near[0].shape
    nothing = jnp.zeros((LANES - 2 * own, cols), jnp.bfloat16)
    right = []
    for m in range(2 * part):
        rows = [nothing, near[m // part][m % part], far[m // part][m % part]]
        right.append(jnp.concatenate(rows, axis=0))
    for core, masked_ref in enumerate((own_ref, other_ref)):
        hold_ref[core] = (early_ref[core] + product(right, masked_ref)).T
    for route in range(count):
        side, core = place_ref[0] ^ (route // 2), place_ref[1] ^ (route % 2)
        for p in range(count):
            start = pl.multiple_of((2 * (p ^ route) + side) * own, own)
            out_ref[route, p * own : (p + 1) * own, :] = hold_ref[
                core, pl.ds(start, own), :
            ].astype(jnp.bfloat16)


def final_terms(place, near, far, masked, early):
    own = near[0].shape[1]
    rows_dev = masked[0].shape[1]
    count = LANES // (2 * own)
    return pl.pallas_call(
        final_kernel,
        out_shape=jax.ShapeDtypeStruct((count, count * own, rows_dev), jnp.bfloat16),
        in_specs=[pl.BlockSpec(memory_space=pltpu.SMEM)] + [WHOLE] * 7,
        out_specs=WHOLE,
        scratch_shapes=[pltpu.VMEM((2, LANES, rows_dev), jnp.float32)],
        compiler_params=SMALL,
        cost_estimate=TINY,
        name="final_terms",
    )(place, *near, *far, *masked, early)


def routed(value, route):
    pairs = []
    for z in range(4):
        for core in range(2):
            to_z = 2 * ((z // 2) ^ (route // 2)) + core
            to_core = (z % 2) ^ (route % 2)
            pairs.append((2 * z + core, 2 * to_z + to_core))
    return lax.ppermute(value, ("ao", "rep"), pairs)


def after(value, *others):
    return lax.optimization_barrier((value,) + others)[0]


def swapped_plan(tensor, mask_rows, occ_green, virt_green, green_mask):
    planes = lax.axis_size("ao")
    steps = range(1, planes)
    z = lax.axis_index("ao")
    core = lax.axis_index("rep")
    aux = lax.axis_index("aux")
    side = lax.axis_index("tpoint")
    own = SL // planes
    half = own // 2
    rows_dev, blocks, cols = tensor.shape
    units = cols // LANES

    def rows_of(plane, part):
        return lax.dynamic_slice_in_dim(tensor, plane * own + part * half, half, 0)

    mine = jnp.where(core == 0, occ_green, virt_green).reshape(-1, blocks, cols)
    whole = lax.dynamic_slice_in_dim(tensor, (z ^ 1) * own, own, 0)
    first = swap(jnp.concatenate([whole, mine]), "ao", 1)
    direct = [swap(jnp.concatenate([rows_of(z ^ k, side), mine]), "ao", k) for k in (2, 3)]
    hops = {3: swap(direct[1][:half], "tpoint", 1)}
    hops[2] = swap(direct[0][:half], "tpoint", 1)
    pieces = [lax.dynamic_slice_in_dim(tensor, z * own, own, 0), first]
    for k in (2, 3):
        pieces += [direct[k - 2], hops[k]]
    stacked = jnp.stack([mine, first[own:], direct[0][half:], direct[1][half:]])
    order = jnp.arange(planes) ^ z
    other = swap(stacked, "rep", 1)
    shape = (blocks,) + occ_green.shape[1:]
    mine_all = stacked[order].reshape(shape)
    other_all = other[order].reshape(shape)
    row_mask = jnp.repeat(mask_rows, RB, axis=0).astype(jnp.bfloat16)
    masked = jnp.swapaxes(tensor, 0, 1) * row_mask.T[:, :, None]
    occ_mask, virt_mask = pair_masks(green_mask, mask_rows[0])
    occ = jnp.where(core == 0, mine_all, other_all) * occ_mask[:, :, None, None]
    virt = jnp.where(core == 0, other_all, mine_all) * virt_mask[:, :, None, None]
    place = jnp.arange(AOB)
    source = (
        (z ^ (place // units % planes)) * (AOB // planes)
        + PAIR * (place % units)
        + place // (planes * units)
    )
    select = (source[:, None] == jnp.arange(AOB)[None, :]).astype(jnp.bfloat16)
    occ = jnp.einsum("ai,mkij->mkaj", select, occ)
    occ = jnp.einsum("mkaj,bj->makb", occ, select).reshape(blocks, AOB, -1)
    virt = jnp.stack(
        [
            jnp.pad(virt, ((0, 0), (0, 0), (0, 0), (0, LANES - AOB))),
            jnp.pad(virt, ((0, 0), (0, 0), (0, 0), (LANES - AOB, 0))),
        ],
        axis=2,
    )
    pieces[0], masked = lax.optimization_barrier((pieces[0], masked))
    sums = contract(side, pieces, occ, virt)
    masked = (masked, swap(after(masked, sums[0]), "rep", 1))
    near1, near2 = swap(sums[1], "ao", 1), swap(sums[2], "ao", 2)
    far0, across = swap(sums[0], "aux", 1), swap(sums[1], "aux", 1)
    far1 = swap(across, "ao", 1)
    near3 = [
        swap(after(sums[3], across, masked[1]), "ao", 3),
        swap(after(sums[4], near1, far0), "ao", 3),
    ]
    far2 = swap(near2, "aux", 1)
    far3 = [swap(after(near3[0], far1), "aux", 1), swap(near3[1], "aux", 1)]
    parts = [sums[0], far0, near1, far1, near2, far2]
    early = early_terms(parts, masked)
    place = jnp.stack([(z // 2) ^ aux, (z % 2) ^ core]).astype(jnp.int32)
    leaving = final_terms(place, near3, far3, masked, early)
    total = None
    for route in range(planes):
        term = routed(leaving[route], route).astype(jnp.float32)
        total = term if total is None else total + term
    index = jnp.arange(2 * planes)
    home = index ^ (2 * (2 * (z // 2) + core) + side)
    return total.reshape(2 * planes, half, -1)[home].reshape(SL, -1)


def per_device(tensor, block_mask, occ_green, virt_green, green_mask):
    rows_dev, blocks, cols = tensor.shape
    shard = lax.axis_index(("aux", "rep"))
    per_shard = rows_dev // RB
    planes = lax.axis_size("ao")

    def mask_of(index):
        return lax.dynamic_slice_in_dim(block_mask, index * per_shard, per_shard, 0)

    sizes = tuple(lax.axis_size(axis) for axis in ("tpoint", "ao", "aux", "rep"))
    simple = sizes == (2, 4, 2, 2) and cols * planes == AOB * AOB and SL // planes == 16
    simple = simple and blocks * 16 == LANES and rows_dev % RB == 0 and occ_green.shape[1] == 3
    if simple:
        return swapped_plan(tensor, mask_of(shard), occ_green, virt_green, green_mask)
    return gathered_plan(tensor, mask_of(shard), occ_green, virt_green, green_mask)


def solution(mesh):
    return jax.shard_map(
        per_device,
        mesh=mesh,
        in_specs=(
            P(("aux", "rep"), None, "ao"),
            P(),
            P(("tpoint", "ao"), None, None, None),
            P(("tpoint", "ao"), None, None, None),
            P(),
        ),
        out_specs=P(("tpoint", "ao"), ("aux", "rep")),
        check_vma=False,
    )
```

```python
import functools

import jax
import jax.numpy as jnp
from jax import lax
from jax.experimental import pallas as pl
from jax.experimental.pallas import tpu as pltpu
from jax.sharding import PartitionSpec as P

AOB = 64
RB = 128
SL = 64
LANES = 128
PAIR = LANES // AOB
TINY = pl.CostEstimate(flops=1, bytes_accessed=1, transcendentals=0)


def pair_masks(green_mask, slab_mask):
    blocks, width = green_mask.shape
    reach = (width - 1) // 2
    neighbour = jnp.arange(blocks)[:, None] + jnp.arange(width)[None, :] - reach
    valid = (neighbour >= 0) & (neighbour < blocks)
    near_mask = slab_mask[jnp.clip(neighbour, 0, blocks - 1)]
    pair = jnp.where(valid, green_mask, 0)
    return pair.astype(jnp.bfloat16), (pair * near_mask).astype(jnp.bfloat16)


def gathered_plan(tensor, mask_rows, occ_green, virt_green, green_mask):
    blocks = tensor.shape[1]
    row_mask = jnp.repeat(mask_rows, RB, axis=0).astype(jnp.bfloat16)
    masked = tensor * row_mask[:, :, None]
    reach = (occ_green.shape[1] - 1) // 2
    slab = lax.all_to_all(tensor[:SL], "ao", split_axis=0, concat_axis=2, tiled=True)
    occ_all = lax.all_gather(occ_green, "ao", axis=0, tiled=True)
    virt_all = lax.all_gather(virt_green, "ao", axis=0, tiled=True)
    occ_mask, virt_mask = pair_masks(green_mask, mask_rows[0])
    occ = occ_all * occ_mask[:, :, None, None]
    virt = virt_all * virt_mask[:, :, None, None]
    own = slab.shape[0]
    padded = jnp.pad(slab.reshape(own, blocks, AOB, AOB), ((0, 0), (reach, reach), (0, 0), (0, 0)))
    total = None
    for offset in range(2 * reach + 1):
        near = padded[:, offset : offset + blocks]
        inner = jnp.einsum(
            "rimn,ins->rims", near, virt[:, offset], preferred_element_type=jnp.float32
        ).astype(jnp.bfloat16)
        term = jnp.einsum(
            "ilm,rims->rils", occ[:, offset], inner, preferred_element_type=jnp.float32
        )
        total = term if total is None else total + term
    own_sums = total.astype(jnp.bfloat16).reshape(own, blocks, AOB * AOB)
    back = lax.all_to_all(own_sums, "ao", split_axis=2, concat_axis=0, tiled=True)
    sums = lax.all_gather(back, ("aux", "rep"), axis=0, tiled=True)
    partial_terms = lax.dot_general(
        sums, masked, (((1, 2), (1, 2)), ((), ())), preferred_element_type=jnp.float32
    )
    return lax.psum_scatter(partial_terms, "ao", scatter_dimension=0, tiled=True)


def swap(value, axis, step):
    count = lax.axis_size(axis)
    return lax.ppermute(value, axis, [(i, i ^ step) for i in range(count)])


def contract_kernel(planes, part_ref, *refs):
    pieces = refs[: 2 * planes - 2]
    occ_ref, virt_ref = refs[2 * planes - 2 : 2 * planes]
    outs = refs[2 * planes : 3 * planes + 1]
    even_ref, odd_ref, weight_ref, inner_ref, sums_ref = refs[3 * planes + 1 :]
    blocks, own, cols = outs[0].shape
    width = virt_ref.shape[1]
    reach = (width - 1) // 2
    units = cols // LANES
    pairs = own // PAIR
    rows = planes * units
    f32 = jnp.float32
    for plane in range(planes):
        for p in range(own):
            if plane < 2:
                piece, at = pieces[plane], part_ref[0] * (own // 2) ^ p
            else:
                piece, at = pieces[2 * plane - 2 + p // (own // 2)], p % (own // 2)
            value = piece[at].astype(f32)
            target = even_ref if p % 2 == 0 else odd_ref
            for u in range(units):
                start = (p // 2) * rows + plane * units + u
                target[pl.ds(start, blocks, stride=pairs * rows), :] = value[
                    :, u * LANES : (u + 1) * LANES
                ]
    nothing = jnp.zeros((AOB, LANES), jnp.bfloat16)
    for m in range(blocks):
        for k in range(width):
            if not 0 <= m + k - reach < blocks:
                inner_ref[m, :, k * AOB : (k + 1) * AOB, :] = jnp.zeros(
                    (pairs // 2, AOB, 2 * LANES), jnp.bfloat16
                )
    for j in range(blocks):
        at = slice(j * pairs * rows, (j + 1) * pairs * rows)
        near = jnp.concatenate([even_ref[at, :], odd_ref[at, :]], axis=1).astype(jnp.bfloat16)
        for k in range(width):
            m = j + reach - k
            if not 0 <= m < blocks:
                continue
            for side in range(2):
                block = virt_ref[m, k, side]
                for half in range(2):
                    top = (side * 2 + half) * AOB
                    for out_half in range(2):
                        weight_ref[
                            j, k, top : top + AOB, out_half * LANES : (out_half + 1) * LANES
                        ] = block if half == out_half else nothing
            inner = jnp.dot(near, weight_ref[j, k], preferred_element_type=f32).astype(jnp.bfloat16)
            for pair in range(pairs):
                for half in range(2):
                    top = k * AOB + half * rows
                    inner_ref[
                        m,
                        pair // 2,
                        top : top + rows,
                        (pair % 2) * LANES : (pair % 2 + 1) * LANES,
                    ] = inner[pair * rows : (pair + 1) * rows, half * LANES : (half + 1) * LANES]
    low = lax.broadcasted_iota(jnp.int32, (rows, LANES), 1) < AOB
    for m in range(blocks):
        for group in range(pairs // 2):
            total = jnp.dot(occ_ref[m], inner_ref[m, group], preferred_element_type=f32)
            for side in range(2):
                lanes = slice(side * LANES, (side + 1) * LANES)
                first, second = total[:rows, lanes], total[rows:, lanes]
                even = jnp.where(low, first, pltpu.roll(second, AOB, 1))
                odd = jnp.where(low, pltpu.roll(first, AOB, 1), second)
                for part, value in enumerate((even, odd)):
                    p = (group * 2 + side) * 2 + part
                    for plane in range(planes):
                        start = (m * planes + plane) * units * own + p
                        sums_ref[pl.ds(start, units, stride=own), :] = value[
                            plane * units : (plane + 1) * units
                        ]
        for plane in range(planes):
            for u in range(units):
                start = ((m * planes + plane) * units + u) * own
                into, at = outs[plane], m
                if plane == planes - 1 and m >= blocks // 2:
                    into, at = outs[planes], m - blocks // 2
                into[at, :, u * LANES : (u + 1) * LANES] = sums_ref[
                    start : start + own, :
                ].astype(jnp.bfloat16)


def contract(part, pieces, occ, virt):
    planes = len(pieces) // 2 + 1
    own, blocks, cols = pieces[0].shape
    width = virt.shape[1]
    units = cols // LANES
    pairs = own // PAIR
    rows = planes * units
    whole = pl.BlockSpec(memory_space=pltpu.VMEM)
    return pl.pallas_call(
        functools.partial(contract_kernel, planes),
        out_shape=[jax.ShapeDtypeStruct((blocks, own, cols), jnp.bfloat16)] * (planes - 1)
        + [jax.ShapeDtypeStruct((blocks // 2, own, cols), jnp.bfloat16)] * 2,
        in_specs=[pl.BlockSpec(memory_space=pltpu.SMEM)] + [whole] * (2 * planes),
        out_specs=[whole] * (planes + 1),
        scratch_shapes=[
            pltpu.VMEM((blocks * pairs * rows, LANES), jnp.float32),
            pltpu.VMEM((blocks * pairs * rows, LANES), jnp.float32),
            pltpu.VMEM((blocks, width, 2 * LANES, 2 * LANES), jnp.bfloat16),
            pltpu.VMEM((blocks, pairs // 2, width * AOB, 2 * LANES), jnp.bfloat16),
            pltpu.VMEM((blocks * rows * own, LANES), jnp.float32),
        ],
        compiler_params=pltpu.CompilerParams(vmem_limit_bytes=20 * 1024 * 1024),
        cost_estimate=TINY,
        name="contract_slab",
    )(part.reshape(1), *pieces, occ, virt)


def add_product(right, rows_ref, keep_ref, core, into_ref):
    for block in range(rows_ref.shape[1] // RB):
        at = slice(block * RB, (block + 1) * RB)
        total = into_ref[core, at, :]
        for m in range(rows_ref.shape[0]):
            term = lax.dot_general(
                rows_ref[m, at, :],
                right[m],
                (((1,), (1,)), ((), ())),
                preferred_element_type=jnp.float32,
            )
            total = total + term * keep_ref[core, block, m]
        into_ref[core, at, :] = total


WHOLE = pl.BlockSpec(memory_space=pltpu.VMEM)
SMALL = pltpu.CompilerParams(vmem_limit_bytes=16 * 1024 * 1024)


def early_kernel(count, keep_ref, *refs):
    parts, sources, out_ref = refs[:count], refs[count : count + 2], refs[count + 2]
    kept, sem = refs[count + 3 : count + 5], refs[count + 5]
    copies = [pltpu.make_async_copy(sources[c], kept[c], sem.at[c]) for c in range(2)]
    for copy in copies:
        copy.start()
    blocks, own, cols = parts[0].shape
    nothing = jnp.zeros((LANES - count * own, cols), jnp.bfloat16)
    right = []
    for m in range(blocks):
        right.append(jnp.concatenate([part[m] for part in parts] + [nothing], axis=0))
    out_ref[...] = jnp.zeros_like(out_ref)
    for core in range(2):
        copies[core].wait()
        add_product(right, kept[core], keep_ref, core, out_ref)


def early_terms(keep, parts, rows):
    rows_dev = rows[0].shape[1]
    return pl.pallas_call(
        functools.partial(early_kernel, len(parts)),
        out_shape=[jax.ShapeDtypeStruct((2, rows_dev, LANES), jnp.float32)]
        + [pltpu.VMEM(value.shape, value.dtype) for value in rows],
        in_specs=[pl.BlockSpec(memory_space=pltpu.SMEM)]
        + [WHOLE] * len(parts)
        + [pl.BlockSpec(memory_space=pl.ANY)] * 2,
        out_specs=[WHOLE] * 3,
        scratch_shapes=[pltpu.SemaphoreType.DMA((2,))],
        compiler_params=SMALL,
        cost_estimate=TINY,
        name="early_terms",
    )(keep, *parts, *rows)


def final_kernel(place_ref, keep_ref, *refs):
    near, far = refs[:2], refs[2:4]
    own_ref, other_ref, early_ref, out_ref, sum_ref, hold_ref = refs[4:]
    count = out_ref.shape[0]
    part, own, cols = near[0].shape
    nothing = jnp.zeros((LANES - 2 * own, cols), jnp.bfloat16)
    right = []
    for m in range(2 * part):
        rows = [nothing, near[m // part][m % part], far[m // part][m % part]]
        right.append(jnp.concatenate(rows, axis=0))
    sum_ref[...] = early_ref[...]
    for core, rows_ref in enumerate((own_ref, other_ref)):
        add_product(right, rows_ref, keep_ref, core, sum_ref)
        hold_ref[core] = sum_ref[core].T
    for route in range(count):
        side, core = place_ref[0] ^ (route // 2), place_ref[1] ^ (route % 2)
        for p in range(count):
            start = pl.multiple_of((2 * (p ^ route) + side) * own, own)
            out_ref[route, p * own : (p + 1) * own, :] = hold_ref[
                core, pl.ds(start, own), :
            ].astype(jnp.bfloat16)


def final_terms(place, keep, near, far, rows, early):
    own = near[0].shape[1]
    rows_dev = rows[0].shape[1]
    count = LANES // (2 * own)
    return pl.pallas_call(
        final_kernel,
        out_shape=jax.ShapeDtypeStruct((count, count * own, rows_dev), jnp.bfloat16),
        in_specs=[pl.BlockSpec(memory_space=pltpu.SMEM)] * 2 + [WHOLE] * 7,
        out_specs=WHOLE,
        scratch_shapes=[
            pltpu.VMEM((2, rows_dev, LANES), jnp.float32),
            pltpu.VMEM((2, LANES, rows_dev), jnp.float32),
        ],
        compiler_params=SMALL,
        cost_estimate=TINY,
        name="final_terms",
    )(place, keep, *near, *far, *rows, early)


def routed(value, route):
    pairs = []
    for z in range(4):
        for core in range(2):
            to_z = 2 * ((z // 2) ^ (route // 2)) + core
            to_core = (z % 2) ^ (route % 2)
            pairs.append((2 * z + core, 2 * to_z + to_core))
    return lax.ppermute(value, ("ao", "rep"), pairs)


def after(value, *others):
    return lax.optimization_barrier((value,) + others)[0]


def swapped_plan(tensor, mask_rows, other_mask_rows, occ_green, virt_green, green_mask):
    planes = lax.axis_size("ao")
    steps = range(1, planes)
    z = lax.axis_index("ao")
    core = lax.axis_index("rep")
    aux = lax.axis_index("aux")
    side = lax.axis_index("tpoint")
    own = SL // planes
    half = own // 2
    rows_dev, blocks, cols = tensor.shape
    units = cols // LANES

    def rows_of(plane, part):
        return lax.dynamic_slice_in_dim(tensor, plane * own + part * half, half, 0)

    mine = jnp.where(core == 0, occ_green, virt_green).reshape(-1, blocks, cols)
    whole = lax.dynamic_slice_in_dim(tensor, (z ^ 1) * own, own, 0)
    leaving = [jnp.concatenate([rows_of(z ^ k, side), mine]) for k in (2, 3)]
    first = swap(after(jnp.concatenate([whole, mine]), *leaving), "ao", 1)
    direct = [swap(leaving[0], "ao", 2)]
    direct.append(swap(after(leaving[1], direct[0]), "ao", 3))
    rows = jnp.swapaxes(after(tensor, direct[0]), 0, 1)
    direct[1], rows = lax.optimization_barrier((direct[1], rows))
    hops = {2: swap(direct[0][:half], "tpoint", 1)}
    hops[3] = swap(after(direct[1][:half], hops[2]), "tpoint", 1)
    pieces = [lax.dynamic_slice_in_dim(tensor, z * own, own, 0), first]
    for k in (2, 3):
        pieces += [direct[k - 2], hops[k]]
    stacked = jnp.stack([mine, first[own:], direct[0][half:], direct[1][half:]])
    order = jnp.arange(planes) ^ z
    other = swap(stacked, "rep", 1)
    shape = (blocks,) + occ_green.shape[1:]
    mine_all = stacked[order].reshape(shape)
    other_all = other[order].reshape(shape)
    occ_mask, virt_mask = pair_masks(green_mask, mask_rows[0])
    occ = jnp.where(core == 0, mine_all, other_all) * occ_mask[:, :, None, None]
    virt = jnp.where(core == 0, other_all, mine_all) * virt_mask[:, :, None, None]
    place = jnp.arange(AOB)
    source = (
        (z ^ (place // units % planes)) * (AOB // planes)
        + PAIR * (place % units)
        + place // (planes * units)
    )
    select = (source[:, None] == jnp.arange(AOB)[None, :]).astype(jnp.bfloat16)
    occ = jnp.einsum("ai,mkij->mkaj", select, occ)
    occ = jnp.einsum("mkaj,bj->makb", occ, select).reshape(blocks, AOB, -1)
    virt = jnp.stack(
        [
            jnp.pad(virt, ((0, 0), (0, 0), (0, 0), (0, LANES - AOB))),
            jnp.pad(virt, ((0, 0), (0, 0), (0, 0), (LANES - AOB, 0))),
        ],
        axis=2,
    )
    sums = contract(side, pieces, occ, virt)
    rows = (rows, swap(after(rows, sums[0]), "rep", 1))
    near1, near2 = swap(sums[1], "ao", 1), swap(sums[2], "ao", 2)
    far0, across = swap(sums[0], "aux", 1), swap(sums[1], "aux", 1)
    far1 = swap(across, "ao", 1)
    near3 = [
        swap(after(sums[3], across), "ao", 3),
        swap(after(sums[4], near1, far0), "ao", 3),
    ]
    far2 = swap(near2, "aux", 1)
    far3 = [swap(after(near3[0], far1), "aux", 1), swap(near3[1], "aux", 1)]
    parts = [sums[0], far0, near1, far1, near2, far2]
    keep = jnp.stack([mask_rows, other_mask_rows]).astype(jnp.float32)
    early, *rows = early_terms(keep, parts, rows)
    place = jnp.stack([(z // 2) ^ aux, (z % 2) ^ core]).astype(jnp.int32)
    leaving = final_terms(place, keep, near3, far3, rows, early)
    total = None
    for route in range(planes):
        term = routed(leaving[route], route).astype(jnp.float32)
        total = term if total is None else total + term
    index = jnp.arange(2 * planes)
    home = index ^ (2 * (2 * (z // 2) + core) + side)
    return total.reshape(2 * planes, half, -1)[home].reshape(SL, -1)


def per_device(tensor, block_mask, occ_green, virt_green, green_mask):
    rows_dev, blocks, cols = tensor.shape
    shard = lax.axis_index(("aux", "rep"))
    per_shard = rows_dev // RB
    planes = lax.axis_size("ao")

    def mask_of(index):
        return lax.dynamic_slice_in_dim(block_mask, index * per_shard, per_shard, 0)

    sizes = tuple(lax.axis_size(axis) for axis in ("tpoint", "ao", "aux", "rep"))
    simple = sizes == (2, 4, 2, 2) and cols * planes == AOB * AOB and SL // planes == 16
    simple = simple and blocks * 16 == LANES and rows_dev % RB == 0 and occ_green.shape[1] == 3
    if simple:
        masks = mask_of(shard), mask_of(shard ^ 1)
        return swapped_plan(tensor, *masks, occ_green, virt_green, green_mask)
    return gathered_plan(tensor, mask_of(shard), occ_green, virt_green, green_mask)


def solution(mesh):
    return jax.shard_map(
        per_device,
        mesh=mesh,
        in_specs=(
            P(("aux", "rep"), None, "ao"),
            P(),
            P(("tpoint", "ao"), None, None, None),
            P(("tpoint", "ao"), None, None, None),
            P(),
        ),
        out_specs=P(("tpoint", "ao"), ("aux", "rep")),
        check_vma=False,
    )
```
